32 devices in a mesh: slab: 2 (over y), tm: 4 (over z), chan: 4 (over x, core).
Axes of the slice: x: 2, y: 2, z: 4, core: 2. Of those that a mesh axis runs over, the one named last changes fastest.
Arguments:
- record: bfloat16 [128, 4096], P('chan', ('slab', 'tm')), parts along dimension 1, may hold values from -6 to 6
- quality: int32 [128], P('chan'), may hold values 0 or 1
- fir_taps: float32 [129], replicated, may hold values from -0.5 to 0.5
- source_channels: int32 [128], replicated, may hold values from 0 to 127, as said below
Outputs:
- correlations: float32 [256, 128, 512], P(('slab', 'tm'), 'chan'), parts along dimension 0
The draws below stay inside these ranges and needn't reach their ends.
There are 2 independent parts, one for each index of `slab`. The reference program is written for one: setup_inputs(seed, part) draws one part's arguments, and reference() takes and returns one part's arrays. A program takes and returns all parts, laid end to end along the dimension named above; an argument that names none is the same for every part. Nothing has to cross between parts.
Inputs may be any that keep to these rules, and one draw needn't show every extreme that they name: `source_channels`: distinct channel numbers.
All inputs are finite; a program needn't handle non-finite values. No bound on the sum of `quality` on one device may be relied on, other than what follows from the above.
Results may differ from the reference program's by a relative error of at most 0.0055.
Values may be sent and summed in bfloat16 or wider, within the bound.
A program may use at most 64 MiB of HBM per device.

```python
import math
import jax
import jax.numpy as jnp
from jax import lax

PANEL = 128
HALF = 256
FIRH = 64
T_DEV = 512
TIME = 2048
CHANNELS = 128
N_TM = 4


def draw_source_channels(key, part):
    first_key = jax.random.fold_in(key, 11)
    second_key = jax.random.fold_in(key, 12)
    inner = 1 + jax.random.permutation(first_key, CHANNELS - 2)[:PANEL - 2]
    chosen = jnp.concatenate([jnp.array([0, CHANNELS - 1], dtype=jnp.int32), inner.astype(jnp.int32)])
    return jax.random.permutation(second_key, chosen).astype(jnp.int32)


def with_ends(values, own_key, smallest, top_value):
    longest = values.shape.index(max(values.shape))
    spots = []
    for shift in (0, 1):
        where = [jax.random.randint(jax.random.fold_in(own_key, axis), (), 0, length) for axis, length in enumerate(values.shape)]
        where[longest] = (where[longest] + shift) % values.shape[longest]
        spots.append(tuple(where))
    return values.at[spots[0]].set(smallest).at[spots[1]].set(top_value)


def shard_levels(stream_key, dims, split, low, high):
    def one(position, blocks):
        steps = jax.random.uniform(jax.random.fold_in(jax.random.fold_in(stream_key, 6), position), (blocks,), jnp.float32, low / len(split), high / len(split))
        return jnp.repeat(jnp.exp(steps), dims[position] // blocks).reshape((-1,) + (1,) * (len(dims) - position - 1))

    loudness = one(*split[0])
    for cut in split[1:]:
        loudness = loudness * one(*cut)
    return loudness


def noise(key, shape, deviation, limit, cuts=(), kind=jnp.bfloat16):
    factor_of = shard_levels(key, shape, cuts, -0.22, 0.18) if cuts else 1.0
    drawn = jax.random.normal(key, shape, jnp.float32) * deviation * factor_of
    return jnp.minimum(jnp.maximum(drawn, -limit), limit).astype(kind)


def setup_inputs(seed: int = 0, part: int = 0) -> dict:
    streams_of = jax.random.split(jax.random.key(seed), 5)
    part_keys = jax.random.split(jax.random.fold_in(streams_of[4], part), 5)
    return {
        "record": noise(part_keys[0], (CHANNELS, TIME), 1.0, 6.0, ((0, 4), (1, 4))),
        "quality": with_ends((jax.random.randint(streams_of[1], (CHANNELS,), 0, 8) < 7).astype(jnp.int32), jax.random.fold_in(streams_of[1], 1), 0, 1),
        "fir_taps": noise(streams_of[2], (2 * FIRH + 1,), (2 * FIRH + 1) ** -0.5, 0.5, (), jnp.float32),
        "source_channels": draw_source_channels(jax.random.fold_in(streams_of[4], 71), part),
    }


def whiten_rows(record, fir_taps, quality):
    reach = (fir_taps.shape[0] - 1) // 2
    padded = jnp.pad(record.astype(jnp.float32), ((0, 0), (reach, reach)))
    filtered = lax.conv_general_dilated(padded[:, None, :], fir_taps.astype(jnp.float32)[None, None, :], (1,), 'VALID', precision=lax.Precision.HIGHEST)
    return (filtered[:, 0, :] * quality.astype(jnp.float32)[:, None]).astype(jnp.bfloat16)

def reference(record, quality, fir_taps, source_channels):
    whitened = whiten_rows(record, fir_taps, quality)
    panel = whitened[source_channels]
    scale = 1.0 / math.sqrt(TIME)
    padded = jnp.pad(whitened, ((0, 0), (HALF, HALF)))

    def one_block(total, index):
        start = (index * T_DEV).astype(jnp.int32)
        sources = lax.dynamic_slice_in_dim(panel, start, T_DEV, 1).astype(jnp.float32)
        window = lax.dynamic_slice_in_dim(padded, start, T_DEV + 2 * HALF, 1).astype(jnp.float32)
        lagged = lax.conv_general_dilated(window[:, None, :], sources[:, None, :], (1,), 'VALID', precision=lax.Precision.HIGHEST)
        partial_value = jnp.transpose(lagged[:, :, :2 * HALF], (1, 0, 2)) * scale
        rounded = lax.optimization_barrier(partial_value.astype(jnp.bfloat16)).astype(jnp.float32)
        return (total + rounded, index)
    initial = jnp.zeros((PANEL, CHANNELS, 2 * HALF), jnp.float32)
    result = lax.scan(one_block, initial, jnp.arange(N_TM, dtype=jnp.int32))
    return result[0]
```

```python
import functools
import math

import jax
import jax.numpy as jnp
from jax import lax
from jax.experimental import pallas as pl
from jax.experimental.pallas import tpu as pltpu
from jax.sharding import PartitionSpec as P

HALF = 256
LAGS = 2 * HALF
BLK = 128
PAD = 256
MESH = pl.DeviceIdType.MESH
NT = (((1,), (1,)), ((), ()))


def gather_kernel(n_tm, n_chan, rec_ref, keep_ref, out_ref, s_tm, r_tm, s_x, r_x, s_c, r_c):
    me_t = lax.axis_index("tm")
    me_c = lax.axis_index("chan")
    n_x = n_chan // 2
    core = lax.rem(me_c, 2)
    me_x = me_c // 2
    sibling = me_c + 1 - 2 * core

    def tm_peer(d):
        return {"tm": lax.rem(me_t + d, n_tm)}

    def x_peer(e):
        return {"chan": 2 * lax.rem(me_x + e, n_x) + core}

    barrier = pltpu.get_barrier_semaphore()
    peers = [tm_peer(d) for d in range(1, n_tm)] + [x_peer(e) for e in range(1, n_x)]
    peers.append({"chan": sibling})
    for peer in peers:
        pl.semaphore_signal(barrier, inc=1, device_id=peer, device_id_type=MESH)

    rows = rec_ref.shape[0]
    keep = jnp.broadcast_to(keep_ref[...].astype(jnp.float32), (rows, rows))
    first = lax.broadcasted_iota(jnp.int32, (rows, rows), 0)
    second = lax.broadcasted_iota(jnp.int32, (rows, rows), 1)
    diagonal = jnp.where(first == second, keep, 0.0).astype(jnp.bfloat16)
    out_ref[me_c, me_t] = jnp.dot(
        diagonal, rec_ref[...], preferred_element_type=jnp.float32
    ).astype(jnp.bfloat16)
    pl.semaphore_wait(barrier, len(peers))

    def slot(e, d):
        return out_ref.at[2 * lax.rem(me_x + n_x - e, n_x) + core, lax.rem(me_t + n_tm - d, n_tm)]

    def other_slot(e, d):
        return out_ref.at[
            2 * lax.rem(me_x + n_x - e, n_x) + 1 - core, lax.rem(me_t + n_tm - d, n_tm)
        ]

    def copy(ref, send, recv, peer):
        return pltpu.make_async_remote_copy(
            src_ref=ref, dst_ref=ref, send_sem=send, recv_sem=recv, device_id=peer,
            device_id_type=MESH,
        )

    sent = []

    def start(op):
        op.start()
        sent.append(op)

    def to_x(d):
        for e in range(1, n_x):
            start(copy(slot(0, d), s_x.at[e, d], r_x.at[e, d], x_peer(e)))

    def to_core(e, d):
        start(copy(slot(e, d), s_c.at[e, d], r_c.at[e, d], {"chan": sibling}))

    for d in range(n_tm - 1, 0, -1):
        start(copy(slot(0, 0), s_tm.at[d], r_tm.at[d], tm_peer(d)))
    to_x(0)
    to_core(0, 0)

    def from_x(d):
        for e in range(1, n_x):
            copy(slot(e, d), s_x.at[e, d], r_x.at[e, d], x_peer(e)).wait_recv()
            to_core(e, d)

    for d in range(1, n_tm):
        copy(slot(0, d), s_tm.at[d], r_tm.at[d], tm_peer(d)).wait_recv()
        to_x(d)
        to_core(0, d)
        from_x(d - 1)
    from_x(n_tm - 1)
    for e in range(n_x):
        for d in range(n_tm):
            copy(other_slot(e, d), s_c.at[e, d], r_c.at[e, d], {"chan": sibling}).wait_recv()
    for op in sent:
        op.wait_send()


def three_parts(value):
    high = value.astype(jnp.bfloat16)
    rest = value - high.astype(jnp.float32)
    middle = rest.astype(jnp.bfloat16)
    low = (rest - middle.astype(jnp.float32)).astype(jnp.bfloat16)
    return high, middle, low


def correlate_kernel(
    n_src, all_ref, taps_ref, src_ref, out_ref, taps_row, raw, rev, lhs, rhs_a, rhs_b
):
    n_chan, n_tm, rows, t_dev = all_ref.shape
    total = n_tm * t_dev
    n_ch = n_chan * rows
    panel_rows = src_ref.shape[1]
    padded_src = raw.shape[0] - rows
    blocks = total // BLK + 4
    wide = 2 * BLK
    window = 4 * BLK
    me_t = lax.axis_index("tm")
    me_c = lax.axis_index("chan")
    scale = 1.0 / math.sqrt(total)

    n_taps = taps_ref.shape[1]
    taps_row[...] = jnp.zeros_like(taps_row)
    taps_row[0:1, 0:n_taps] = taps_ref[...]
    spread = jnp.broadcast_to(taps_row[0:1, :], (wide, window))
    forward = pltpu.roll(spread, 64, 1, stride=1, stride_axis=0)
    shifted = pltpu.roll(spread, 65, 1, stride=1, stride_axis=0)
    flip = (
        lax.broadcasted_iota(jnp.int32, (wide, wide), 0)
        + lax.broadcasted_iota(jnp.int32, (wide, wide), 1)
        == wide - 1
    ).astype(jnp.float32).astype(jnp.bfloat16)
    forward_parts = three_parts(forward)
    backward_parts = [
        jnp.dot(flip, part, preferred_element_type=jnp.float32).astype(jnp.bfloat16)
        for part in three_parts(shifted)
    ]

    which = (
        lax.broadcasted_iota(jnp.int32, (n_ch, panel_rows), 0)
        == jnp.broadcast_to(src_ref[...], (n_ch, panel_rows))
    ).astype(jnp.float32).astype(jnp.bfloat16)
    mine = (
        lax.broadcasted_iota(jnp.int32, (padded_src, panel_rows), 0) + me_t * n_src
        == lax.broadcasted_iota(jnp.int32, (padded_src, panel_rows), 1)
    ).astype(jnp.float32).astype(jnp.bfloat16)
    selector = lax.dot_general(
        mine, which, NT, preferred_element_type=jnp.float32
    ).astype(jnp.bfloat16)

    raw[:, 0:PAD] = jnp.zeros((rows + padded_src, PAD), jnp.bfloat16)
    raw[:, PAD + total :] = jnp.zeros((rows + padded_src, PAD), jnp.bfloat16)
    for t in range(n_tm):
        at = slice(PAD + t * t_dev, PAD + (t + 1) * t_dev)
        raw[0:rows, at] = all_ref[me_c, t]
        raw[rows:, at] = jnp.dot(
            selector, all_ref[:, t].reshape(n_ch, t_dev), preferred_element_type=jnp.float32
        ).astype(jnp.bfloat16)

    def filtered(windows, parts):
        return sum(
            lax.dot_general(windows, part, NT, preferred_element_type=jnp.float32)
            for part in parts
        )

    lhs[...] = jnp.zeros_like(lhs)
    n_wide = total // wide
    group = 8
    for q0 in range(0, n_wide, group):
        windows = jnp.concatenate(
            [
                raw[0:rows, PAD + wide * q - BLK : PAD + wide * q - BLK + window]
                for q in range(q0, q0 + group)
            ],
            axis=0,
        )
        values = filtered(windows, forward_parts).astype(jnp.bfloat16)
        for i in range(group):
            for j in range(4):
                begin = BLK * (3 - j) + wide * (q0 + i)
                lhs[j * rows : (j + 1) * rows, begin : begin + wide] = values[
                    i * rows : (i + 1) * rows
                ]

    rev[:, 0:wide] = jnp.zeros((padded_src, wide), jnp.float32)
    end = wide * (n_wide + 2)
    rev[:, end:] = jnp.zeros((padded_src, rev.shape[1] - end), jnp.float32)
    for q0 in range(1, n_wide + 2, group):
        qs = range(q0, min(q0 + group, n_wide + 2))
        windows = jnp.concatenate(
            [
                raw[rows:, PAD + total - wide * q : PAD + total - wide * q + window]
                for q in qs
            ],
            axis=0,
        )
        values = filtered(windows, backward_parts).astype(jnp.bfloat16).astype(jnp.float32)
        for i, q in enumerate(qs):
            place = lax.broadcasted_iota(jnp.int32, (padded_src, wide), 1) + wide * q
            inside = (place >= 3 * BLK + 1) & (place <= total + 3 * BLK)
            rev[:, wide * q : wide * (q + 1)] = jnp.where(
                inside, values[i * padded_src : (i + 1) * padded_src], 0.0
            )

    width = BLK * (blocks + 1)

    def build(ref, pair):
        for h in range(2):
            row = rev[pl.ds(2 * pair + h, 1), 0:width]
            spread = jnp.broadcast_to(row, (16, width))
            steps = pltpu.roll(spread, 0, 1, stride=1, stride_axis=0)
            for k in range(8):
                moved = steps if k == 0 else pltpu.roll(steps, 16 * k, 1)
                moved = moved.astype(jnp.bfloat16)
                for m in range(blocks):
                    base = BLK * (blocks - m)
                    ref[BLK * m + 16 * k : BLK * m + 16 * (k + 1), BLK * h : BLK * (h + 1)] = (
                        moved[:, base : base + BLK]
                    )

    def multiply(ref, pair):
        result = jnp.dot(lhs[...], ref[...], preferred_element_type=jnp.float32) * scale
        for h in range(2):
            for j in range(4):
                out_ref[2 * pair + h, :, BLK * j : BLK * (j + 1)] = result[
                    j * rows : (j + 1) * rows, BLK * h : BLK * (h + 1)
                ]

    pairs = n_src // 2
    build(rhs_a, 0)

    def step(i, carry):
        multiply(rhs_a, 2 * i)
        build(rhs_b, 2 * i + 1)
        multiply(rhs_b, 2 * i + 1)
        build(rhs_a, jnp.minimum(2 * i + 2, pairs - 1))
        return carry

    lax.fori_loop(0, pairs // 2, step, 0)


def local(record, quality, fir_taps, source_channels):
    rows, t_dev = record.shape
    n_tm = lax.axis_size("tm")
    n_chan = lax.axis_size("chan")
    panel_rows = source_channels.shape[0]
    n_src = panel_rows // n_tm
    total = t_dev * n_tm
    blocks = total // BLK + 4
    vmem = pl.BlockSpec(memory_space=pltpu.VMEM)
    dma = pltpu.SemaphoreType.DMA
    everything = pl.pallas_call(
        functools.partial(gather_kernel, n_tm, n_chan),
        out_shape=jax.ShapeDtypeStruct((n_chan, n_tm, rows, t_dev), jnp.bfloat16),
        in_specs=[vmem] * 2,
        out_specs=vmem,
        scratch_shapes=[
            dma((n_tm,)),
            dma((n_tm,)),
            dma((n_chan // 2, n_tm)),
            dma((n_chan // 2, n_tm)),
            dma((n_chan // 2, n_tm)),
            dma((n_chan // 2, n_tm)),
        ],
        compiler_params=pltpu.CompilerParams(
            collective_id=0, has_side_effects=True, vmem_limit_bytes=32 * 2**20
        ),
        name="gather_records",
    )(record, quality.reshape(1, rows))
    padded_src = -(-n_src // 16) * 16
    return pl.pallas_call(
        functools.partial(correlate_kernel, n_src),
        out_shape=jax.ShapeDtypeStruct((n_src, rows, LAGS), jnp.float32),
        in_specs=[vmem] * 3,
        out_specs=vmem,
        scratch_shapes=[
            pltpu.VMEM((8, 4 * BLK), jnp.float32),
            pltpu.VMEM((rows + padded_src, total + 2 * PAD), jnp.bfloat16),
            pltpu.VMEM((padded_src, BLK * (blocks + 2)), jnp.float32),
            pltpu.VMEM((4 * rows, BLK * blocks), jnp.bfloat16),
            pltpu.VMEM((BLK * blocks, 2 * BLK), jnp.bfloat16),
            pltpu.VMEM((BLK * blocks, 2 * BLK), jnp.bfloat16),
        ],
        compiler_params=pltpu.CompilerParams(vmem_limit_bytes=56 * 2**20),
        name="correlate_all",
    )(everything, fir_taps.reshape(1, -1), source_channels.reshape(1, -1))


def solution(mesh):
    placed = (P("chan", ("slab", "tm")), P("chan"), P(), P())
    return jax.shard_map(
        local,
        mesh=mesh,
        in_specs=placed,
        out_specs=P(("slab", "tm"), "chan", None),
        check_vma=False,
    )
```

```python
import functools
import math

import jax
import jax.numpy as jnp
from jax import lax
from jax.experimental import pallas as pl
from jax.experimental.pallas import tpu as pltpu
from jax.sharding import PartitionSpec as P

HALF = 256
LAGS = 2 * HALF
BLK = 128
PAD = 256
MESH = pl.DeviceIdType.MESH
NT = (((1,), (1,)), ((), ()))


def three_parts(value):
    high = value.astype(jnp.bfloat16)
    rest = value - high.astype(jnp.float32)
    middle = rest.astype(jnp.bfloat16)
    low = (rest - middle.astype(jnp.float32)).astype(jnp.bfloat16)
    return high, middle, low


def prepare_kernel(
    n_src, n_tm, n_chan, rec_hbm, keep_hbm, taps_hbm, src_hbm, lhs, rev,
    out_ref, rec_ref, keep_ref, taps_ref, src_ref, taps_row, raw, forward_ref, backward_ref,
    l_sem, s_tm, r_tm, s_x, r_x, s_c, r_c,
):
    pairs = ((rec_hbm, rec_ref), (keep_hbm, keep_ref), (taps_hbm, taps_ref), (src_hbm, src_ref))
    loads = [pltpu.make_async_copy(a, b, l_sem.at[i]) for i, (a, b) in enumerate(pairs)]
    for load in loads:
        load.start()
    me_t = lax.axis_index("tm")
    me_c = lax.axis_index("chan")
    n_x = n_chan // 2
    core = lax.rem(me_c, 2)
    me_x = me_c // 2
    sibling = me_c + 1 - 2 * core

    def tm_peer(d):
        return {"tm": lax.rem(me_t + d, n_tm)}

    def x_peer(e):
        return {"chan": 2 * lax.rem(me_x + e, n_x) + core}

    barrier = pltpu.get_barrier_semaphore()
    peers = [tm_peer(d) for d in range(1, n_tm)] + [x_peer(e) for e in range(1, n_x)]
    peers.append({"chan": sibling})
    for peer in peers:
        pl.semaphore_signal(barrier, inc=1, device_id=peer, device_id_type=MESH)

    rows, t_dev = rec_ref.shape
    total = n_tm * t_dev
    n_ch = n_chan * rows
    panel_rows = src_ref.shape[1]
    padded_src = raw.shape[0] - rows
    wide = 2 * BLK
    window = 4 * BLK
    loads[0].wait()
    loads[1].wait()
    keep = jnp.broadcast_to(keep_ref[...].astype(jnp.float32), (rows, rows))
    first = lax.broadcasted_iota(jnp.int32, (rows, rows), 0)
    second = lax.broadcasted_iota(jnp.int32, (rows, rows), 1)
    diagonal = jnp.where(first == second, keep, 0.0).astype(jnp.bfloat16)
    out_ref[me_c, me_t] = jnp.dot(
        diagonal, rec_ref[...], preferred_element_type=jnp.float32
    ).astype(jnp.bfloat16)
    pl.semaphore_wait(barrier, len(peers))

    def slot(e, d):
        return out_ref.at[2 * lax.rem(me_x + n_x - e, n_x) + core, lax.rem(me_t + n_tm - d, n_tm)]

    def other_slot(e, d):
        return out_ref.at[
            2 * lax.rem(me_x + n_x - e, n_x) + 1 - core, lax.rem(me_t + n_tm - d, n_tm)
        ]

    def copy(ref, send, recv, peer):
        return pltpu.make_async_remote_copy(
            src_ref=ref, dst_ref=ref, send_sem=send, recv_sem=recv, device_id=peer,
            device_id_type=MESH,
        )

    sent = []

    def start(op):
        op.start()
        sent.append(op)

    def to_x(d):
        for e in range(1, n_x):
            start(copy(slot(0, d), s_x.at[e, d], r_x.at[e, d], x_peer(e)))

    def to_core(e, d):
        start(copy(slot(e, d), s_c.at[e, d], r_c.at[e, d], {"chan": sibling}))

    for d in range(n_tm - 1, 0, -1):
        start(copy(slot(0, 0), s_tm.at[d], r_tm.at[d], tm_peer(d)))
    to_x(0)
    to_core(0, 0)

    loads[2].wait()
    loads[3].wait()
    n_taps = taps_ref.shape[1]
    taps_row[...] = jnp.zeros_like(taps_row)
    taps_row[0:1, 0:n_taps] = taps_ref[...]
    spread = jnp.broadcast_to(taps_row[0:1, :], (wide, window))
    forward = pltpu.roll(spread, 64, 1, stride=1, stride_axis=0)
    shifted = pltpu.roll(spread, 65, 1, stride=1, stride_axis=0)
    flip = (
        lax.broadcasted_iota(jnp.int32, (wide, wide), 0)
        + lax.broadcasted_iota(jnp.int32, (wide, wide), 1)
        == wide - 1
    ).astype(jnp.float32).astype(jnp.bfloat16)
    for i, part in enumerate(three_parts(forward)):
        forward_ref[i] = part
    for i, part in enumerate(three_parts(shifted)):
        backward_ref[i] = jnp.dot(flip, part, preferred_element_type=jnp.float32).astype(
            jnp.bfloat16
        )

    which = (
        lax.broadcasted_iota(jnp.int32, (n_ch, panel_rows), 0)
        == jnp.broadcast_to(src_ref[...], (n_ch, panel_rows))
    ).astype(jnp.float32).astype(jnp.bfloat16)
    mine = (
        lax.broadcasted_iota(jnp.int32, (padded_src, panel_rows), 0) + me_t * n_src
        == lax.broadcasted_iota(jnp.int32, (padded_src, panel_rows), 1)
    ).astype(jnp.float32).astype(jnp.bfloat16)
    selector = lax.dot_general(
        mine, which, NT, preferred_element_type=jnp.float32
    ).astype(jnp.bfloat16)

    raw[:, 0:PAD] = jnp.zeros((rows + padded_src, PAD), jnp.bfloat16)
    raw[:, PAD + total :] = jnp.zeros((rows + padded_src, PAD), jnp.bfloat16)
    lhs[...] = jnp.zeros_like(lhs)

    def filtered(windows, parts):
        return sum(
            lax.dot_general(windows, parts[i], NT, preferred_element_type=jnp.float32)
            for i in range(3)
        )

    def from_x(d):
        for e in range(1, n_x):
            copy(slot(e, d), s_x.at[e, d], r_x.at[e, d], x_peer(e)).wait_recv()
            to_core(e, d)

    for d in range(1, n_tm):
        copy(slot(0, d), s_tm.at[d], r_tm.at[d], tm_peer(d)).wait_recv()
        to_x(d)
        to_core(0, d)
        from_x(d - 1)
    for t in range(n_tm):
        raw[0:rows, PAD + t * t_dev : PAD + (t + 1) * t_dev] = out_ref[me_c, t]
    n_wide = total // wide
    group = 8
    for q0 in range(0, n_wide, group):
        windows = jnp.concatenate(
            [
                raw[0:rows, PAD + wide * q - BLK : PAD + wide * q - BLK + window]
                for q in range(q0, q0 + group)
            ],
            axis=0,
        )
        values = filtered(windows, forward_ref).astype(jnp.bfloat16)
        for i in range(group):
            for j in range(4):
                begin = BLK * (3 - j) + wide * (q0 + i)
                lhs[j * rows : (j + 1) * rows, begin : begin + wide] = values[
                    i * rows : (i + 1) * rows
                ]

    from_x(n_tm - 1)
    for e in range(n_x):
        for d in range(n_tm):
            copy(other_slot(e, d), s_c.at[e, d], r_c.at[e, d], {"chan": sibling}).wait_recv()
    for t in range(n_tm):
        raw[rows:, PAD + t * t_dev : PAD + (t + 1) * t_dev] = jnp.dot(
            selector, out_ref[:, t].reshape(n_ch, t_dev), preferred_element_type=jnp.float32
        ).astype(jnp.bfloat16)
    rev[:, 0:wide] = jnp.zeros((padded_src, wide), jnp.float32)
    end = wide * (n_wide + 2)
    rev[:, end:] = jnp.zeros((padded_src, rev.shape[1] - end), jnp.float32)
    for q0 in range(1, n_wide + 2, group):
        qs = range(q0, min(q0 + group, n_wide + 2))
        windows = jnp.concatenate(
            [
                raw[rows:, PAD + total - wide * q : PAD + total - wide * q + window]
                for q in qs
            ],
            axis=0,
        )
        values = filtered(windows, backward_ref).astype(jnp.bfloat16).astype(jnp.float32)
        for i, q in enumerate(qs):
            place = lax.broadcasted_iota(jnp.int32, (padded_src, wide), 1) + wide * q
            inside = (place >= 3 * BLK + 1) & (place <= total + 3 * BLK)
            rev[:, wide * q : wide * (q + 1)] = jnp.where(
                inside, values[i * padded_src : (i + 1) * padded_src], 0.0
            )

    for op in sent:
        op.wait_send()


def correlate_kernel(n_src, total, lhs, rev, out_ref, rhs_a, rhs_b):
    rows = out_ref.shape[1]
    blocks = total // BLK + 4
    scale = 1.0 / math.sqrt(total)
    width = BLK * (blocks + 1)

    def build(ref, pair):
        for h in range(2):
            row = rev[pl.ds(2 * pair + h, 1), 0:width]
            spread = jnp.broadcast_to(row, (16, width))
            steps = pltpu.roll(spread, 0, 1, stride=1, stride_axis=0)
            for k in range(8):
                moved = steps if k == 0 else pltpu.roll(steps, 16 * k, 1)
                moved = moved.astype(jnp.bfloat16)
                for m in range(blocks):
                    base = BLK * (blocks - m)
                    ref[BLK * m + 16 * k : BLK * m + 16 * (k + 1), BLK * h : BLK * (h + 1)] = (
                        moved[:, base : base + BLK]
                    )

    def multiply(ref, pair):
        result = jnp.dot(lhs[...], ref[...], preferred_element_type=jnp.float32) * scale
        for h in range(2):
            for j in range(4):
                out_ref[2 * pair + h, :, BLK * j : BLK * (j + 1)] = result[
                    j * rows : (j + 1) * rows, BLK * h : BLK * (h + 1)
                ]

    pairs = n_src // 2
    build(rhs_a, 0)

    def step(i, carry):
        multiply(rhs_a, 2 * i)
        build(rhs_b, 2 * i + 1)
        multiply(rhs_b, 2 * i + 1)
        build(rhs_a, jnp.minimum(2 * i + 2, pairs - 1))
        return carry

    lax.fori_loop(0, pairs // 2, step, 0)


def local(record, quality, fir_taps, source_channels):
    rows, t_dev = record.shape
    n_tm = lax.axis_size("tm")
    n_chan = lax.axis_size("chan")
    panel_rows = source_channels.shape[0]
    n_src = panel_rows // n_tm
    total = t_dev * n_tm
    blocks = total // BLK + 4
    vmem = pl.BlockSpec(memory_space=pltpu.VMEM)
    dma = pltpu.SemaphoreType.DMA
    padded_src = -(-n_src // 16) * 16
    n_x = n_chan // 2
    hbm = pl.BlockSpec(memory_space=pltpu.HBM)
    lhs, rev = pl.pallas_call(
        functools.partial(prepare_kernel, n_src, n_tm, n_chan),
        out_shape=[
            jax.ShapeDtypeStruct((4 * rows, BLK * blocks), jnp.bfloat16),
            jax.ShapeDtypeStruct((padded_src, BLK * (blocks + 2)), jnp.float32),
        ],
        in_specs=[hbm] * 4,
        out_specs=[vmem] * 2,
        scratch_shapes=[
            pltpu.VMEM((n_chan, n_tm, rows, t_dev), jnp.bfloat16),
            pltpu.VMEM((rows, t_dev), jnp.bfloat16),
            pltpu.VMEM((1, rows), jnp.int32),
            pltpu.VMEM((1, fir_taps.shape[0]), jnp.float32),
            pltpu.VMEM((1, panel_rows), jnp.int32),
            pltpu.VMEM((8, 4 * BLK), jnp.float32),
            pltpu.VMEM((rows + padded_src, total + 2 * PAD), jnp.bfloat16),
            pltpu.VMEM((3, 2 * BLK, 4 * BLK), jnp.bfloat16),
            pltpu.VMEM((3, 2 * BLK, 4 * BLK), jnp.bfloat16),
            dma((4,)),
            dma((n_tm,)),
            dma((n_tm,)),
            dma((n_x, n_tm)),
            dma((n_x, n_tm)),
            dma((n_x, n_tm)),
            dma((n_x, n_tm)),
        ],
        compiler_params=pltpu.CompilerParams(
            collective_id=0, has_side_effects=True, vmem_limit_bytes=40 * 2**20
        ),
        name="gather_and_filter",
    )(record, quality.reshape(1, -1), fir_taps.reshape(1, -1), source_channels.reshape(1, -1))
    return pl.pallas_call(
        functools.partial(correlate_kernel, n_src, total),
        out_shape=jax.ShapeDtypeStruct((n_src, rows, LAGS), jnp.float32),
        in_specs=[vmem] * 2,
        out_specs=vmem,
        scratch_shapes=[
            pltpu.VMEM((BLK * blocks, 2 * BLK), jnp.bfloat16),
            pltpu.VMEM((BLK * blocks, 2 * BLK), jnp.bfloat16),
        ],
        compiler_params=pltpu.CompilerParams(vmem_limit_bytes=40 * 2**20),
        name="correlate_all",
    )(lhs, rev)


def solution(mesh):
    placed = (P("chan", ("slab", "tm")), P("chan"), P(), P())
    return jax.shard_map(
        local,
        mesh=mesh,
        in_specs=placed,
        out_specs=P(("slab", "tm"), "chan", None),
        check_vma=False,
    )
```

```python
import functools
import math

import jax
import jax.numpy as jnp
from jax import lax
from jax.experimental import pallas as pl
from jax.experimental.pallas import tpu as pltpu
from jax.sharding import PartitionSpec as P

HALF = 256
LAGS = 2 * HALF
BLK = 128
PAD = 256
MESH = pl.DeviceIdType.MESH
NT = (((1,), (1,)), ((), ()))


def three_parts(value):
    high = value.astype(jnp.bfloat16)
    rest = value - high.astype(jnp.float32)
    middle = rest.astype(jnp.bfloat16)
    low = (rest - middle.astype(jnp.float32)).astype(jnp.bfloat16)
    return high, middle, low


def prepare_kernel(
    n_src, n_tm, n_chan, rec_hbm, keep_hbm, taps_hbm, src_hbm, lhs, rev,
    out_ref, rec_ref, keep_ref, taps_ref, src_ref, taps_row, raw, forward_ref, backward_ref,
    l_sem, s_tm, r_tm, s_x, r_x, s_c, r_c,
):
    pairs = ((rec_hbm, rec_ref), (keep_hbm, keep_ref), (taps_hbm, taps_ref), (src_hbm, src_ref))
    loads = [pltpu.make_async_copy(a, b, l_sem.at[i]) for i, (a, b) in enumerate(pairs)]
    for load in loads:
        load.start()
    me_t = lax.axis_index("tm")
    me_c = lax.axis_index("chan")
    n_x = n_chan // 2
    core = lax.rem(me_c, 2)
    me_x = me_c // 2
    sibling = me_c + 1 - 2 * core

    def tm_peer(d):
        return {"tm": lax.rem(me_t + d, n_tm)}

    def x_peer(e):
        return {"chan": 2 * lax.rem(me_x + e, n_x) + core}

    barrier = pltpu.get_barrier_semaphore()
    peers = [tm_peer(d) for d in range(1, n_tm)] + [x_peer(e) for e in range(1, n_x)]
    peers.append({"chan": sibling})
    for peer in peers:
        pl.semaphore_signal(barrier, inc=1, device_id=peer, device_id_type=MESH)

    rows, t_dev = rec_ref.shape
    total = n_tm * t_dev
    n_ch = n_chan * rows
    panel_rows = src_ref.shape[1]
    padded_src = raw.shape[0] - rows
    wide = 2 * BLK
    window = 4 * BLK
    loads[0].wait()
    loads[1].wait()
    keep = jnp.broadcast_to(keep_ref[...].astype(jnp.float32), (rows, rows))
    first = lax.broadcasted_iota(jnp.int32, (rows, rows), 0)
    second = lax.broadcasted_iota(jnp.int32, (rows, rows), 1)
    diagonal = jnp.where(first == second, keep, 0.0).astype(jnp.bfloat16)
    out_ref[me_c, me_t] = jnp.dot(
        diagonal, rec_ref[...], preferred_element_type=jnp.float32
    ).astype(jnp.bfloat16)
    pl.semaphore_wait(barrier, len(peers))

    def slot(e, d):
        return out_ref.at[2 * lax.rem(me_x + n_x - e, n_x) + core, lax.rem(me_t + n_tm - d, n_tm)]

    def other_slot(e, d):
        return out_ref.at[
            2 * lax.rem(me_x + n_x - e, n_x) + 1 - core, lax.rem(me_t + n_tm - d, n_tm)
        ]

    def copy(ref, send, recv, peer):
        return pltpu.make_async_remote_copy(
            src_ref=ref, dst_ref=ref, send_sem=send, recv_sem=recv, device_id=peer,
            device_id_type=MESH,
        )

    sent = []

    def start(op):
        op.start()
        sent.append(op)

    def to_x(d):
        for e in range(1, n_x):
            start(copy(slot(0, d), s_x.at[e, d], r_x.at[e, d], x_peer(e)))

    def to_core(e, d):
        start(copy(slot(e, d), s_c.at[e, d], r_c.at[e, d], {"chan": sibling}))

    for d in range(n_tm - 1, 0, -1):
        start(copy(slot(0, 0), s_tm.at[d], r_tm.at[d], tm_peer(d)))
    to_x(0)
    to_core(0, 0)

    loads[2].wait()
    loads[3].wait()
    n_taps = taps_ref.shape[1]
    taps_row[...] = jnp.zeros_like(taps_row)
    taps_row[0:1, 0:n_taps] = taps_ref[...]
    spread = jnp.broadcast_to(taps_row[0:1, :], (wide, window))
    forward = pltpu.roll(spread, 64, 1, stride=1, stride_axis=0)
    shifted = pltpu.roll(spread, 65, 1, stride=1, stride_axis=0)
    flip = (
        lax.broadcasted_iota(jnp.int32, (wide, wide), 0)
        + lax.broadcasted_iota(jnp.int32, (wide, wide), 1)
        == wide - 1
    ).astype(jnp.float32).astype(jnp.bfloat16)
    for i, part in enumerate(three_parts(forward)):
        forward_ref[i] = part
    for i, part in enumerate(three_parts(shifted)):
        backward_ref[i] = jnp.dot(flip, part, preferred_element_type=jnp.float32).astype(
            jnp.bfloat16
        )

    which = (
        lax.broadcasted_iota(jnp.int32, (n_ch, panel_rows), 0)
        == jnp.broadcast_to(src_ref[...], (n_ch, panel_rows))
    ).astype(jnp.float32).astype(jnp.bfloat16)
    mine = (
        lax.broadcasted_iota(jnp.int32, (padded_src, panel_rows), 0) + me_t * n_src
        == lax.broadcasted_iota(jnp.int32, (padded_src, panel_rows), 1)
    ).astype(jnp.float32).astype(jnp.bfloat16)
    selector = lax.dot_general(
        mine, which, NT, preferred_element_type=jnp.float32
    ).astype(jnp.bfloat16)

    raw[:, 0:PAD] = jnp.zeros((rows + padded_src, PAD), jnp.bfloat16)
    raw[:, PAD + total :] = jnp.zeros((rows + padded_src, PAD), jnp.bfloat16)
    lhs[...] = jnp.zeros_like(lhs)

    def filtered(windows, parts):
        return sum(
            lax.dot_general(windows, parts[i], NT, preferred_element_type=jnp.float32)
            for i in range(3)
        )

    def from_x(d):
        for e in range(1, n_x):
            copy(slot(e, d), s_x.at[e, d], r_x.at[e, d], x_peer(e)).wait_recv()
            to_core(e, d)

    for d in range(1, n_tm):
        copy(slot(0, d), s_tm.at[d], r_tm.at[d], tm_peer(d)).wait_recv()
        to_x(d)
        to_core(0, d)
        from_x(d - 1)
    for t in range(n_tm):
        raw[0:rows, PAD + t * t_dev : PAD + (t + 1) * t_dev] = out_ref[me_c, t]
    n_wide = total // wide
    group = 8
    for q0 in range(0, n_wide, group):
        windows = jnp.concatenate(
            [
                raw[0:rows, PAD + wide * q - BLK : PAD + wide * q - BLK + window]
                for q in range(q0, q0 + group)
            ],
            axis=0,
        )
        values = filtered(windows, forward_ref).astype(jnp.bfloat16)
        for i in range(group):
            for j in range(4):
                begin = BLK * (3 - j) + wide * (q0 + i)
                lhs[j * rows : (j + 1) * rows, begin : begin + wide] = values[
                    i * rows : (i + 1) * rows
                ]

    from_x(n_tm - 1)
    for e in range(n_x):
        for d in range(n_tm):
            copy(other_slot(e, d), s_c.at[e, d], r_c.at[e, d], {"chan": sibling}).wait_recv()
    for t in range(n_tm):
        raw[rows:, PAD + t * t_dev : PAD + (t + 1) * t_dev] = jnp.dot(
            selector, out_ref[:, t].reshape(n_ch, t_dev), preferred_element_type=jnp.float32
        ).astype(jnp.bfloat16)
    rev[:, 0:wide] = jnp.zeros((padded_src, wide), jnp.float32)
    end = wide * (n_wide + 2)
    rev[:, end:] = jnp.zeros((padded_src, rev.shape[1] - end), jnp.float32)
    for q0 in range(1, n_wide + 2, group):
        qs = range(q0, min(q0 + group, n_wide + 2))
        windows = jnp.concatenate(
            [
                raw[rows:, PAD + total - wide * q : PAD + total - wide * q + window]
                for q in qs
            ],
            axis=0,
        )
        values = filtered(windows, backward_ref).astype(jnp.bfloat16).astype(jnp.float32)
        for i, q in enumerate(qs):
            place = lax.broadcasted_iota(jnp.int32, (padded_src, wide), 1) + wide * q
            inside = (place >= 3 * BLK + 1) & (place <= total + 3 * BLK)
            rev[:, wide * q : wide * (q + 1)] = jnp.where(
                inside, values[i * padded_src : (i + 1) * padded_src], 0.0
            )

    for op in sent:
        op.wait_send()


def correlate_kernel(n_src, total, lhs, rev, out_ref, rhs_a, rhs_b):
    rows = out_ref.shape[1]
    blocks = total // BLK + 4
    scale = 1.0 / math.sqrt(total)
    width = BLK * (blocks + 1)

    def build(ref, pair):
        for h in range(2):
            row = rev[pl.ds(2 * pair + h, 1), 0:width]
            spread = jnp.broadcast_to(row, (16, width))
            steps = pltpu.roll(spread, 0, 1, stride=1, stride_axis=0)
            for k in range(8):
                moved = steps if k == 0 else pltpu.roll(steps, 16 * k, 1)
                moved = moved.astype(jnp.bfloat16)
                for m in range(blocks):
                    base = BLK * (blocks - m)
                    ref[BLK * m + 16 * k : BLK * m + 16 * (k + 1), BLK * h : BLK * (h + 1)] = (
                        moved[:, base : base + BLK]
                    )

    def multiply(ref, pair):
        result = jnp.dot(lhs[...], ref[...], preferred_element_type=jnp.float32) * scale
        for h in range(2):
            for j in range(4):
                out_ref[2 * pair + h, :, BLK * j : BLK * (j + 1)] = result[
                    j * rows : (j + 1) * rows, BLK * h : BLK * (h + 1)
                ]

    pairs = n_src // 2
    build(rhs_a, 0)

    def step(i, carry):
        multiply(rhs_a, 2 * i)
        build(rhs_b, 2 * i + 1)
        multiply(rhs_b, 2 * i + 1)
        build(rhs_a, jnp.minimum(2 * i + 2, pairs - 1))
        return carry

    lax.fori_loop(0, pairs // 2, step, 0)


def local(record, quality, fir_taps, source_channels):
    rows, t_dev = record.shape
    n_tm = lax.axis_size("tm")
    n_chan = lax.axis_size("chan")
    panel_rows = source_channels.shape[0]
    n_src = panel_rows // n_tm
    total = t_dev * n_tm
    blocks = total // BLK + 4
    vmem = pl.BlockSpec(memory_space=pltpu.VMEM)
    dma = pltpu.SemaphoreType.DMA
    padded_src = -(-n_src // 16) * 16
    n_x = n_chan // 2
    hbm = pl.BlockSpec(memory_space=pltpu.HBM)
    lhs, rev = pl.pallas_call(
        functools.partial(prepare_kernel, n_src, n_tm, n_chan),
        out_shape=[
            jax.ShapeDtypeStruct((4 * rows, BLK * blocks), jnp.bfloat16),
            jax.ShapeDtypeStruct((padded_src, BLK * (blocks + 2)), jnp.float32),
        ],
        in_specs=[hbm] * 4,
        out_specs=[vmem] * 2,
        scratch_shapes=[
            pltpu.VMEM((n_chan, n_tm, rows, t_dev), jnp.bfloat16),
            pltpu.VMEM((rows, t_dev), jnp.bfloat16),
            pltpu.VMEM((1, rows), jnp.int32),
            pltpu.VMEM((1, fir_taps.shape[0]), jnp.float32),
            pltpu.VMEM((1, panel_rows), jnp.int32),
            pltpu.VMEM((8, 4 * BLK), jnp.float32),
            pltpu.VMEM((rows + padded_src, total + 2 * PAD), jnp.bfloat16),
            pltpu.VMEM((3, 2 * BLK, 4 * BLK), jnp.bfloat16),
            pltpu.VMEM((3, 2 * BLK, 4 * BLK), jnp.bfloat16),
            dma((4,)),
            dma((n_tm,)),
            dma((n_tm,)),
            dma((n_x, n_tm)),
            dma((n_x, n_tm)),
            dma((n_x, n_tm)),
            dma((n_x, n_tm)),
        ],
        compiler_params=pltpu.CompilerParams(
            collective_id=0, has_side_effects=True, vmem_limit_bytes=62 * 2**20 + 800 * 2**10
        ),
        name="gather_and_filter",
    )(record, quality.reshape(1, -1), fir_taps.reshape(1, -1), source_channels.reshape(1, -1))
    return pl.pallas_call(
        functools.partial(correlate_kernel, n_src, total),
        out_shape=jax.ShapeDtypeStruct((n_src, rows, LAGS), jnp.float32),
        in_specs=[vmem] * 2,
        out_specs=vmem,
        scratch_shapes=[
            pltpu.VMEM((BLK * blocks, 2 * BLK), jnp.bfloat16),
            pltpu.VMEM((BLK * blocks, 2 * BLK), jnp.bfloat16),
        ],
        compiler_params=pltpu.CompilerParams(vmem_limit_bytes=62 * 2**20 + 800 * 2**10),
        name="correlate_all",
    )(lhs, rev)


def solution(mesh):
    placed = (P("chan", ("slab", "tm")), P("chan"), P(), P())
    return jax.shard_map(
        local,
        mesh=mesh,
        in_specs=placed,
        out_specs=P(("slab", "tm"), "chan", None),
        check_vma=False,
    )
```
